32 devices in a mesh: row: 8 (over z, y), col: 4 (over x, core).
Axes of the slice: x: 2, y: 2, z: 4, core: 2. Of those that a mesh axis runs over, the one named last changes fastest.
Arguments:
- rhs: bfloat16 [8, 4, 64, 768], P('row', 'col'), may hold values from -6 to 6
- operator_blocks: bfloat16 [8, 4, 768, 768], P('row', 'col'), may hold values from -0.5 to 3.5
- local_solver: bfloat16 [8, 4, 768, 768], P('row', 'col'), may hold values from -0.1 to 0.6
- modes: bfloat16 [8, 4, 48, 768], P('row', 'col'), may hold values from -0.21875 to 0.21875
- coupling: bfloat16 [8, 4, 4, 128, 128], P('row', 'col'), may hold values from -0.25 to 0.25
- coarse_inverse: bfloat16 [4, 384, 8, 192], P('col', None, 'row'), may hold values from -0.05 to 0.15
- send_block: int32 [8, 4, 8], P('row', 'col'), may hold values from 0 to 5
- slot_dir: int32 [8, 4, 4], P('row', 'col'), may hold values from -1 to 7, as said below
- slot_block: int32 [8, 4, 4], P('row', 'col'), may hold values from 0 to 5
Outputs:
- solution: float32 [8, 4, 64, 768], P('row', 'col')
The draws below stay inside these ranges and needn't reach their ends.
Inputs may be any that keep to these rules, and one draw needn't show every extreme that they name: `slot_dir`: each subdomain lists 2 to 4 distinct directions toward subdomains inside the grid in its first slots; the remaining slots hold -1.
All inputs are finite; a program needn't handle non-finite values.
Results may differ from the reference program's by a relative error of at most 0.0033.
Values may be sent and summed in bfloat16 or wider, within the bound.
A program may use at most 64 MiB of HBM per device.

```python
import jax
import jax.numpy as jnp
from jax import lax

SUB = 768
BLK = 128
NBLK = 6
MODES = 48
COLS = 64
SLOTS = 4
NDIR = 8
ITERS = 6
GRID_ROWS = 8
GRID_COLS = 4


def diagonal_values(key):
    uniform_part = jax.random.uniform(jax.random.fold_in(key, 21), (GRID_ROWS, GRID_COLS, SUB), jnp.float32, 0.0, 1.0)
    return jnp.exp(uniform_part * jnp.log(3.0))


def identity_mask():
    return (jnp.arange(SUB)[:, None] == jnp.arange(SUB)[None, :]).astype(jnp.float32)


def draw_operator_blocks(key, part):
    diagonal = diagonal_values(key)
    shape = (GRID_ROWS, GRID_COLS, SUB, SUB)
    noise = jax.random.normal(jax.random.fold_in(key, 22), shape, jnp.float32) * 0.015
    return (noise + identity_mask() * diagonal[..., :, None]).astype(jnp.bfloat16)


def draw_local_solver(key, part):
    diagonal = diagonal_values(key)
    shape = (GRID_ROWS, GRID_COLS, SUB, SUB)
    noise = jax.random.normal(jax.random.fold_in(key, 23), shape, jnp.float32) * 0.0025
    return (noise + identity_mask() * (0.5 / diagonal)[..., :, None]).astype(jnp.bfloat16)


def draw_coarse_inverse(key, part):
    shape = (GRID_COLS, GRID_ROWS * MODES, GRID_ROWS, GRID_COLS * MODES)
    col_in = jnp.arange(GRID_COLS)[:, None, None, None]
    row_in = (jnp.arange(GRID_ROWS * MODES) // MODES)[None, :, None, None]
    mode_in = (jnp.arange(GRID_ROWS * MODES) % MODES)[None, :, None, None]
    row_out = jnp.arange(GRID_ROWS)[None, None, :, None]
    col_out = (jnp.arange(GRID_COLS * MODES) // MODES)[None, None, None, :]
    mode_out = (jnp.arange(GRID_COLS * MODES) % MODES)[None, None, None, :]
    aligned = (row_in == row_out) & (mode_in == mode_out)
    same = aligned & (col_in == col_out)
    after = aligned & (col_in == (col_out + 1) % GRID_COLS)
    before = aligned & (col_in == (col_out + GRID_COLS - 1) % GRID_COLS)
    noise = jax.random.normal(jax.random.fold_in(key, 31), shape, jnp.float32) * 0.0025
    structured = same.astype(jnp.float32) * 0.1 + (after | before).astype(jnp.float32) * 0.08
    return (noise + structured).astype(jnp.bfloat16)


def draw_slot_dir(key, part):
    rows = jnp.arange(GRID_ROWS)[:, None, None]
    cols = jnp.arange(GRID_COLS)[None, :, None]
    offset_a = jnp.array([-1, -1, -1, 0, 0, 1, 1, 1], jnp.int32)[None, None, :]
    offset_b = jnp.array([-1, 0, 1, -1, 1, -1, 0, 1], jnp.int32)[None, None, :]
    valid = (rows + offset_a >= 0) & (rows + offset_a < GRID_ROWS) & (cols + offset_b >= 0) & (cols + offset_b < GRID_COLS)
    scores = jax.random.randint(jax.random.fold_in(key, 41), (GRID_ROWS, GRID_COLS, NDIR), 0, 1 << 20) * NDIR + jnp.arange(NDIR)
    scores = jnp.where(valid, scores, -1)
    order = jnp.argsort(-scores, axis=-1, stable=True).astype(jnp.int32)
    valid_count = jnp.sum(valid.astype(jnp.int32), axis=-1)
    listed = jax.random.randint(jax.random.fold_in(key, 42), (GRID_ROWS, GRID_COLS), 2, SLOTS + 1)
    forced = (jnp.arange(GRID_ROWS)[:, None] + jnp.arange(GRID_COLS)[None, :]) % 3 == 0
    listed = jnp.where(forced, SLOTS, listed)
    listed = jnp.minimum(listed, valid_count)
    taken = order[..., :SLOTS]
    return jnp.where(jnp.arange(SLOTS)[None, None, :] < listed[..., None], taken, -1).astype(jnp.int32)


def place_ends(values, own_key, smallest, top_value):
    index_at = [jax.random.randint(jax.random.fold_in(own_key, axis), (), 0, length) for axis, length in enumerate(values.shape)]
    longest = values.shape.index(max(values.shape))
    beside = index_at[:longest] + [(index_at[longest] + 1) % values.shape[longest]] + index_at[longest + 1:]
    return values.at[tuple(index_at)].set(smallest).at[tuple(beside)].set(top_value)


def block_scale(key, shape, split, smallest, largest):
    def one(position, shards_of):
        steps = jax.random.uniform(jax.random.fold_in(jax.random.fold_in(key, 6), position), (shards_of,), jnp.float32, smallest / len(split), largest / len(split))
        return jnp.repeat(jnp.exp(steps), shape[position] // shards_of).reshape((-1,) + (1,) * (len(shape) - position - 1))

    loudness = one(*split[0])
    for cut in split[1:]:
        loudness = loudness * one(*cut)
    return loudness


def gaussian(key, dims, width, bound, pieces=(), held_as=jnp.bfloat16):
    gain = block_scale(key, dims, pieces, -0.22, 0.18) if pieces else 1.0
    values = jax.random.normal(key, dims, jnp.float32) * width * gain
    return jnp.minimum(jnp.maximum(values, -bound), bound).astype(held_as)


def setup_inputs(seed: int = 0) -> dict:
    splits = jax.random.split(jax.random.key(seed), 10)
    return {
        "rhs": gaussian(splits[0], (GRID_ROWS, GRID_COLS, COLS, SUB), 1.0, 6.0, ((0, 8), (1, 4))),
        "operator_blocks": draw_operator_blocks(jax.random.fold_in(splits[9], 71), 0),
        "local_solver": draw_local_solver(jax.random.fold_in(splits[9], 71), 0),
        "modes": gaussian(splits[3], (GRID_ROWS, GRID_COLS, MODES, SUB), SUB ** -0.5, 0.21875, ((0, 8), (1, 4))),
        "coupling": gaussian(splits[4], (GRID_ROWS, GRID_COLS, SLOTS, BLK, BLK), (4 * BLK) ** -0.5, 0.25, ((0, 8), (1, 4))),
        "coarse_inverse": draw_coarse_inverse(jax.random.fold_in(splits[9], 71), 0),
        "send_block": place_ends(jax.random.randint(splits[6], (GRID_ROWS, GRID_COLS, NDIR), 0, NBLK), jax.random.fold_in(splits[6], 1), 0, NBLK - 1).astype(jnp.int32),
        "slot_dir": draw_slot_dir(jax.random.fold_in(splits[9], 71), 0),
        "slot_block": place_ends(jax.random.randint(splits[8], (GRID_ROWS, GRID_COLS, SLOTS), 0, NBLK), jax.random.fold_in(splits[8], 1), 0, NBLK - 1).astype(jnp.int32),
    }


OFFSETS = ((-1, -1), (-1, 0), (-1, 1), (0, -1), (0, 1), (1, -1), (1, 0), (1, 1))


def reference(rhs, operator_blocks, local_solver, modes, coupling, coarse_inverse, send_block, slot_dir, slot_block):
    highest = lax.Precision.HIGHEST
    subdomains = GRID_ROWS * GRID_COLS
    rhs_full = rhs.astype(jnp.float32)
    flat_operator = operator_blocks.reshape(subdomains, SUB, SUB)
    flat_solver = local_solver.reshape(subdomains, SUB, SUB)
    send_onehot = (send_block[..., None] == jnp.arange(NBLK)).astype(jnp.float32)
    dir_onehot = (slot_dir[..., None] == jnp.arange(NDIR)).astype(jnp.float32)
    block_onehot = (slot_block[..., None] == jnp.arange(NBLK)).astype(jnp.float32)
    coupling_full = coupling.astype(jnp.float32)
    modes_full = modes.astype(jnp.float32)

    def local_product(field_half, matrices):
        def one_block(pair):
            return jnp.dot(pair[0], pair[1], preferred_element_type=jnp.float32)
        result = lax.map(one_block, (field_half.reshape(subdomains, COLS, SUB), matrices))
        return result.reshape(GRID_ROWS, GRID_COLS, COLS, SUB)

    def apply_operator(field_half):
        blocks = field_half.astype(jnp.float32).reshape(GRID_ROWS, GRID_COLS, COLS, NBLK, BLK)
        outgoing = jnp.einsum("abckn,abek->abecn", blocks, send_onehot, precision=highest)
        padded = jnp.pad(outgoing, ((1, 1), (1, 1), (0, 0), (0, 0), (0, 0)))
        arrived = []
        for direction in range(NDIR):
            shift_a, shift_b = OFFSETS[direction]
            arrived.append(padded[1 + shift_a:1 + shift_a + GRID_ROWS, 1 + shift_b:1 + shift_b + GRID_COLS, NDIR - 1 - direction])
        incoming = jnp.stack(arrived, axis=2)
        chosen = jnp.einsum("absd,abdcn->abscn", dir_onehot, incoming, precision=highest)
        coupled = jnp.einsum("abscn,absnm->abscm", chosen, coupling_full, precision=highest)
        placed = jnp.einsum("abscm,absk->abckm", coupled, block_onehot, precision=highest)
        return local_product(field_half, flat_operator) + placed.reshape(GRID_ROWS, GRID_COLS, COLS, SUB)

    def coarse_solve(rounded):
        restricted = jnp.einsum("abms,abcs->abmc", modes_full, rounded.astype(jnp.float32), precision=highest)
        restricted = restricted.astype(jnp.bfloat16)
        inputs = jnp.transpose(restricted, (1, 0, 2, 3)).reshape(GRID_COLS, GRID_ROWS * MODES, COLS)

        def accumulate(total, pair):
            vector, slab = pair
            product = lax.dot_general(vector, slab.reshape(GRID_ROWS * MODES, GRID_ROWS * GRID_COLS * MODES), (((0,), (0,)), ((), ())), preferred_element_type=jnp.float32)
            return total + product, None

        start_total = jnp.zeros((COLS, GRID_ROWS * GRID_COLS * MODES), jnp.float32)
        total, unused = lax.scan(accumulate, start_total, (inputs, coarse_inverse))
        total = jnp.transpose(total.reshape(COLS, GRID_ROWS, GRID_COLS, MODES), (1, 2, 3, 0))
        return total.astype(jnp.bfloat16)

    def prolong(coarse_half):
        return jnp.einsum("abmc,abms->abcs", coarse_half.astype(jnp.float32), modes_full, precision=highest)

    solution = jnp.zeros((GRID_ROWS, GRID_COLS, COLS, SUB), jnp.float32)
    pending = None
    for iteration in range(ITERS):
        if iteration == 0:
            residual = rhs_full
        else:
            residual = rhs_full - apply_operator(solution.astype(jnp.bfloat16))
        rounded = residual.astype(jnp.bfloat16)
        update = local_product(rounded, flat_solver)
        fresh = None
        if iteration + 1 < ITERS:
            fresh = coarse_solve(rounded)
        if pending is not None:
            update = update + prolong(pending)
        solution = solution + update
        pending = fresh
    return solution
```

```python
import functools

import jax
import jax.numpy as jnp
from jax import lax
from jax.experimental import pallas as pl
from jax.experimental.pallas import tpu as pltpu
from jax.sharding import PartitionSpec as P

ITERS = 6
OFFSETS = ((-1, -1), (-1, 0), (-1, 1), (0, -1), (0, 1), (1, -1), (1, 0), (1, 1))
MESH = pl.DeviceIdType.MESH
F32 = jnp.float32
BF16 = jnp.bfloat16


def kernel(
    grid_rows,
    grid_cols,
    rhs_hbm,
    operator_hbm,
    solver_hbm,
    modes_hbm,
    coupling_hbm,
    coarse_hbm,
    send_block,
    slot_dir,
    slot_block,
    out_ref,
    rhs_ref,
    operator_ref,
    solver_ref,
    modes_ref,
    coupling_ref,
    coarse_ref,
    placed_ref,
    coarse_t_ref,
    field_ref,
    load_sem,
    halo_send_sem,
    halo_recv_sem,
    gather_send_sem,
    gather_recv_sem,
    sum_send_sem,
    sum_recv_sem,
    *slots,
):
    exchanges = ITERS - 1
    outgoing = slots[0:exchanges]
    incoming = slots[exchanges : 2 * exchanges]
    gathered = slots[2 * exchanges : 3 * exchanges]
    partial = slots[3 * exchanges : 4 * exchanges]
    arrived = slots[4 * exchanges : 5 * exchanges]
    row = lax.axis_index("row")
    col = lax.axis_index("col")
    columns, unknowns = rhs_ref.shape
    slot_count, block_size = coupling_ref.shape[0], coupling_ref.shape[1]
    block_count = unknowns // block_size
    mode_count = modes_ref.shape[0]

    def inside(direction):
        shift_a, shift_b = OFFSETS[direction]
        a, b = row + shift_a, col + shift_b
        return (a >= 0) & (a < grid_rows) & (b >= 0) & (b < grid_cols)

    def neighbour(direction):
        shift_a, shift_b = OFFSETS[direction]
        return (row + shift_a, col + shift_b)

    loads = []
    for i, (source, target) in enumerate(
        (
            (rhs_hbm.at[0, 0], rhs_ref),
            (modes_hbm.at[0, 0], modes_ref),
            (solver_hbm.at[0, 0], solver_ref),
            (operator_hbm.at[0, 0], operator_ref),
            (coarse_hbm, coarse_ref),
            (coupling_hbm.at[0, 0], coupling_ref),
        )
    ):
        load = pltpu.make_async_copy(source, target, load_sem.at[i])
        load.start()
        loads.append(load)

    barrier = pltpu.get_barrier_semaphore()
    row_peers = [lax.rem(row + step, grid_rows) for step in range(1, grid_rows)]
    col_peers = [lax.rem(col + step, grid_cols) for step in range(1, grid_cols)]
    for peer in row_peers:
        pl.semaphore_signal(barrier, inc=1, device_id=(peer, col), device_id_type=MESH)
    for peer in col_peers:
        pl.semaphore_signal(barrier, inc=1, device_id=(row, peer), device_id_type=MESH)
    expected = grid_rows + grid_cols - 2
    for direction in (0, 2, 5, 7):
        there = inside(direction)

        @pl.when(there)
        def _():
            pl.semaphore_signal(
                barrier, inc=1, device_id=neighbour(direction), device_id_type=MESH
            )

        expected = expected + there.astype(jnp.int32)

    def halo_copy(k, direction):
        return pltpu.make_async_remote_copy(
            src_ref=outgoing[k].at[direction],
            dst_ref=incoming[k].at[7 - direction],
            send_sem=halo_send_sem.at[k, direction],
            recv_sem=halo_recv_sem.at[k, 7 - direction],
            device_id=neighbour(direction),
            device_id_type=MESH,
        )

    def halo_arrival(k, direction):
        return pltpu.make_async_remote_copy(
            src_ref=outgoing[k].at[7 - direction],
            dst_ref=incoming[k].at[direction],
            send_sem=halo_send_sem.at[k, 7 - direction],
            recv_sem=halo_recv_sem.at[k, direction],
            device_id=neighbour(direction),
            device_id_type=MESH,
        )

    def gather_copy(k, step, slot):
        peer = lax.rem(row + step, grid_rows)
        return pltpu.make_async_remote_copy(
            src_ref=gathered[k].at[slot],
            dst_ref=gathered[k].at[slot],
            send_sem=gather_send_sem.at[k, step],
            recv_sem=gather_recv_sem.at[k, step],
            device_id=(peer, col),
            device_id_type=MESH,
        )

    def sum_copy(k, step, source, target):
        peer = lax.rem(col + step, grid_cols)
        return pltpu.make_async_remote_copy(
            src_ref=partial[k].at[source],
            dst_ref=arrived[k].at[target],
            send_sem=sum_send_sem.at[k, step],
            recv_sem=sum_recv_sem.at[k, step],
            device_id=(row, peer),
            device_id_type=MESH,
        )

    def restrict(k, rounded):
        restricted = lax.dot_general(
            modes_ref[...], rounded, (((1,), (1,)), ((), ())), preferred_element_type=F32
        )
        gathered[k][row] = restricted.astype(BF16)

    def send_restricted(k):
        for step in range(1, grid_rows):
            gather_copy(k, step, row).start()

    loads[0].wait()
    loads[1].wait()
    rhs = rhs_ref[...]
    restrict(0, rhs)
    for direction in range(8):

        @pl.when(jnp.logical_not(inside(direction)))
        def _():
            for k in range(exchanges):
                incoming[k][direction] = jnp.zeros((columns, block_size), BF16)

    pl.semaphore_wait(barrier, expected)
    send_restricted(0)
    loads[2].wait()
    solution = jnp.dot(rhs, solver_ref[...], preferred_element_type=F32)

    for k in range(exchanges):
        field = solution.astype(BF16)
        for block in range(block_count):
            field_ref[block] = field[:, block * block_size : (block + 1) * block_size]
        for direction in range(8):
            outgoing[k][direction] = field_ref[send_block[0, 0, direction]]
        for direction in range(8):

            @pl.when(inside(direction))
            def _():
                halo_copy(k, direction).start()

        if k == 0:
            loads[3].wait()
            loads[4].wait()
            loads[5].wait()
            coarse_t_ref[...] = coarse_ref[...].T
            for s in range(slot_count):
                used = slot_dir[0, 0, s] >= 0
                for block in range(block_count):
                    here = used & (slot_block[0, 0, s] == block)
                    placed_ref[
                        s * block_size : (s + 1) * block_size,
                        block * block_size : (block + 1) * block_size,
                    ] = jnp.where(here, coupling_ref[s], jnp.zeros_like(coupling_ref[s]))
        product = jnp.dot(field, operator_ref[...], preferred_element_type=F32)

        for step in range(1, grid_rows):
            sender = lax.rem(row + grid_rows - step, grid_rows)
            gather_copy(k, step, sender).wait_recv()
        inputs = gathered[k][...].reshape(grid_rows * mode_count, columns)
        sums = jnp.dot(coarse_t_ref[...], inputs, preferred_element_type=F32)
        partial[k][...] = sums.reshape(grid_cols, mode_count, columns)
        for step in range(1, grid_cols):
            sum_copy(k, step, lax.rem(col + step, grid_cols), col).start()
        arrived[k][col] = partial[k][col]

        for direction in range(8):

            @pl.when(inside(direction))
            def _():
                halo_arrival(k, direction).wait_recv()

        chosen = []
        for s in range(slot_count):
            index = slot_dir[0, 0, s]
            block = incoming[k][jnp.maximum(index, 0)]
            chosen.append(jnp.where(index >= 0, block, jnp.zeros_like(block)))
        coupled = jnp.dot(
            jnp.concatenate(chosen, 1), placed_ref[...], preferred_element_type=F32
        )
        rounded = (rhs_ref[...].astype(F32) - (product + coupled)).astype(BF16)
        if k + 1 < exchanges:
            restrict(k + 1, rounded)
            send_restricted(k + 1)
        local = jnp.dot(rounded, solver_ref[...], preferred_element_type=F32)
        for step in range(1, grid_cols):
            sender = lax.rem(col + grid_cols - step, grid_cols)
            sum_copy(k, step, sender, sender).wait_recv()
        coarse = arrived[k][0]
        for j in range(1, grid_cols):
            coarse = coarse + arrived[k][j]
        correction = lax.dot_general(
            coarse.astype(BF16),
            modes_ref[...],
            (((0,), (0,)), ((), ())),
            preferred_element_type=F32,
        )
        solution = solution + (local + correction)

    out_ref[0, 0] = solution
    for k in range(exchanges):
        for step in range(1, grid_rows):
            gather_copy(k, step, row).wait_send()
        for step in range(1, grid_cols):
            sum_copy(k, step, lax.rem(col + step, grid_cols), col).wait_send()
        for direction in range(8):

            @pl.when(inside(direction))
            def _():
                halo_copy(k, direction).wait_send()


def on_device(
    grid_rows,
    grid_cols,
    rhs,
    operator_blocks,
    local_solver,
    modes,
    coupling,
    coarse_inverse,
    send_block,
    slot_dir,
    slot_block,
):
    columns, unknowns = rhs.shape[2:]
    mode_count = modes.shape[2]
    slot_count, block_size = coupling.shape[2:4]
    block_count = unknowns // block_size
    coarse_tile = coarse_inverse[0, :, 0, :]
    exchanges = ITERS - 1
    blocks = pltpu.VMEM((8, columns, block_size), BF16)
    sums = pltpu.VMEM((grid_cols, mode_count, columns), F32)
    anywhere = pl.BlockSpec(memory_space=pl.ANY)
    scalars = pl.BlockSpec(memory_space=pltpu.SMEM)
    return pl.pallas_call(
        functools.partial(kernel, grid_rows, grid_cols),
        out_shape=jax.ShapeDtypeStruct((1, 1, columns, unknowns), F32),
        in_specs=[anywhere] * 6 + [scalars] * 3,
        out_specs=pl.BlockSpec(memory_space=pltpu.VMEM),
        scratch_shapes=[
            pltpu.VMEM((columns, unknowns), BF16),
            pltpu.VMEM((unknowns, unknowns), BF16),
            pltpu.VMEM((unknowns, unknowns), BF16),
            pltpu.VMEM((mode_count, unknowns), BF16),
            pltpu.VMEM((slot_count, block_size, block_size), BF16),
            pltpu.VMEM(coarse_tile.shape, BF16),
            pltpu.VMEM((slot_count * block_size, unknowns), BF16),
            pltpu.VMEM(coarse_tile.shape[::-1], BF16),
            pltpu.VMEM((block_count, columns, block_size), BF16),
            pltpu.SemaphoreType.DMA((6,)),
            pltpu.SemaphoreType.DMA((exchanges, 8)),
            pltpu.SemaphoreType.DMA((exchanges, 8)),
            pltpu.SemaphoreType.DMA((exchanges, grid_rows)),
            pltpu.SemaphoreType.DMA((exchanges, grid_rows)),
            pltpu.SemaphoreType.DMA((exchanges, grid_cols)),
            pltpu.SemaphoreType.DMA((exchanges, grid_cols)),
        ]
        + [blocks] * (2 * exchanges)
        + [pltpu.VMEM((grid_rows, mode_count, columns), BF16)] * exchanges
        + [sums] * (2 * exchanges),
        compiler_params=pltpu.CompilerParams(
            collective_id=0, has_side_effects=True, vmem_limit_bytes=40 * 1024 * 1024
        ),
    )(
        rhs,
        operator_blocks,
        local_solver,
        modes,
        coupling,
        coarse_tile,
        send_block,
        slot_dir,
        slot_block,
    )


def solution(mesh):
    in_specs = (
        P("row", "col", None, None),
        P("row", "col", None, None),
        P("row", "col", None, None),
        P("row", "col", None, None),
        P("row", "col", None, None, None),
        P("col", None, "row", None),
        P("row", "col", None),
        P("row", "col", None),
        P("row", "col", None),
    )
    return jax.shard_map(
        functools.partial(on_device, mesh.shape["row"], mesh.shape["col"]),
        mesh=mesh,
        in_specs=in_specs,
        out_specs=P("row", "col", None, None),
        check_vma=False,
    )
```

```python
import functools

import jax
import jax.numpy as jnp
from jax import lax
from jax.experimental import pallas as pl
from jax.experimental.pallas import tpu as pltpu
from jax.sharding import PartitionSpec as P

ITERS = 6
OFFSETS = ((-1, -1), (-1, 0), (-1, 1), (0, -1), (0, 1), (1, -1), (1, 0), (1, 1))
MESH = pl.DeviceIdType.MESH
F32 = jnp.float32
BF16 = jnp.bfloat16


def kernel(
    grid_rows,
    grid_cols,
    rhs_hbm,
    operator_hbm,
    solver_hbm,
    modes_hbm,
    coupling_hbm,
    coarse_hbm,
    send_block,
    slot_dir,
    slot_block,
    out_ref,
    rhs_ref,
    operator_ref,
    solver_ref,
    modes_ref,
    coupling_ref,
    coarse_ref,
    placed_ref,
    field_ref,
    partial_ref,
    load_sem,
    halo_send_sem,
    halo_recv_sem,
    gather_send_sem,
    gather_recv_sem,
    sum_send_sem,
    sum_recv_sem,
    *slots,
):
    exchanges = ITERS - 1
    outgoing = slots[0:exchanges]
    incoming = slots[exchanges : 2 * exchanges]
    gathered = slots[2 * exchanges : 3 * exchanges]
    parting = slots[3 * exchanges : 4 * exchanges]
    arrived = slots[4 * exchanges : 5 * exchanges]
    row = lax.axis_index("row")
    col = lax.axis_index("col")
    columns, unknowns = rhs_ref.shape
    slot_count, block_size = coupling_ref.shape[0], coupling_ref.shape[1]
    block_count = unknowns // block_size
    mode_count = modes_ref.shape[0]

    def inside(direction):
        shift_a, shift_b = OFFSETS[direction]
        a, b = row + shift_a, col + shift_b
        return (a >= 0) & (a < grid_rows) & (b >= 0) & (b < grid_cols)

    def neighbour(direction):
        shift_a, shift_b = OFFSETS[direction]
        return (row + shift_a, col + shift_b)

    loads = []
    for i, (source, target) in enumerate(
        (
            (rhs_hbm.at[0, 0], rhs_ref),
            (modes_hbm.at[0, 0], modes_ref),
            (solver_hbm.at[0, 0], solver_ref),
            (operator_hbm.at[0, 0], operator_ref),
            (coarse_hbm, coarse_ref),
            (coupling_hbm.at[0, 0], coupling_ref),
        )
    ):
        load = pltpu.make_async_copy(source, target, load_sem.at[i])
        load.start()
        loads.append(load)

    barrier = pltpu.get_barrier_semaphore()

    def around(index, size):
        steps = sorted(range(1, size), key=lambda step: -min(step, size - step))
        peers = [index + step for step in steps]
        return [jnp.where(peer >= size, peer - size, peer) for peer in peers]

    row_peers = around(row, grid_rows)
    col_peers = around(col, grid_cols)
    col_slots = sorted(range(grid_cols - 1), key=lambda at: -min(at + 1, grid_cols - 1 - at))
    for peer in row_peers:
        pl.semaphore_signal(barrier, inc=1, device_id=(peer, col), device_id_type=MESH)
    for peer in col_peers:
        pl.semaphore_signal(barrier, inc=1, device_id=(row, peer), device_id_type=MESH)
    expected = grid_rows + grid_cols - 2
    for direction in (0, 2, 5, 7):
        there = inside(direction)

        @pl.when(there)
        def _():
            pl.semaphore_signal(
                barrier, inc=1, device_id=neighbour(direction), device_id_type=MESH
            )

        expected = expected + there.astype(jnp.int32)

    def halo_copy(k, direction):
        return pltpu.make_async_remote_copy(
            src_ref=outgoing[k].at[direction],
            dst_ref=incoming[k].at[7 - direction],
            send_sem=halo_send_sem.at[direction],
            recv_sem=halo_recv_sem.at[k, 7 - direction],
            device_id=neighbour(direction),
            device_id_type=MESH,
        )

    def halo_arrival(k, direction):
        return pltpu.make_async_remote_copy(
            src_ref=outgoing[k].at[7 - direction],
            dst_ref=incoming[k].at[direction],
            send_sem=halo_send_sem.at[7 - direction],
            recv_sem=halo_recv_sem.at[k, direction],
            device_id=neighbour(direction),
            device_id_type=MESH,
        )

    def gather_copy(k, peer, slot):
        return pltpu.make_async_remote_copy(
            src_ref=gathered[k].at[slot],
            dst_ref=gathered[k].at[slot],
            send_sem=gather_send_sem.at[k],
            recv_sem=gather_recv_sem.at[k],
            device_id=(peer, col),
            device_id_type=MESH,
        )

    def sum_copy(k, peer, source, slot):
        return pltpu.make_async_remote_copy(
            src_ref=parting[k].at[source],
            dst_ref=arrived[k].at[slot],
            send_sem=sum_send_sem.at[k],
            recv_sem=sum_recv_sem.at[k],
            device_id=(row, peer),
            device_id_type=MESH,
        )

    def all_gathers(k):
        return gather_copy(k, row_peers[0], pl.ds(0, grid_rows - 1))

    def all_sums(k):
        both = pl.ds(0, grid_cols - 1)
        return sum_copy(k, col_peers[0], both, both)

    def restrict(k, rounded):
        restricted = lax.dot_general(
            modes_ref[...], rounded, (((1,), (1,)), ((), ())), preferred_element_type=F32
        )
        gathered[k][row] = restricted.astype(BF16)

    def send_restricted(k):
        for peer in row_peers:
            gather_copy(k, peer, row).start()

    loads[0].wait()
    loads[1].wait()
    rhs = rhs_ref[...]
    restrict(0, rhs)
    for direction in range(8):

        @pl.when(jnp.logical_not(inside(direction)))
        def _():
            for k in range(exchanges):
                incoming[k][direction] = jnp.zeros((columns, block_size), BF16)

    pl.semaphore_wait(barrier, expected)
    send_restricted(0)
    loads[2].wait()
    solution = jnp.dot(rhs, solver_ref[...], preferred_element_type=F32)

    for k in range(exchanges):
        field = solution.astype(BF16)
        for block in range(block_count):
            field_ref[block] = field[:, block * block_size : (block + 1) * block_size]
        for direction in range(8):
            outgoing[k][direction] = field_ref[send_block[0, 0, direction]]
        for direction in (0, 2, 5, 7, 1, 6, 3, 4):

            @pl.when(inside(direction))
            def _():
                halo_copy(k, direction).start()

        if k == 0:
            loads[3].wait()
            loads[4].wait()
            loads[5].wait()
            for s in range(slot_count):
                used = slot_dir[0, 0, s] >= 0
                for block in range(block_count):
                    here = used & (slot_block[0, 0, s] == block)
                    placed_ref[
                        s * block_size : (s + 1) * block_size,
                        block * block_size : (block + 1) * block_size,
                    ] = jnp.where(here, coupling_ref[s], jnp.zeros_like(coupling_ref[s]))
        product = jnp.dot(field, operator_ref[...], preferred_element_type=F32)

        all_gathers(k).wait_recv()
        inputs = gathered[k][...].reshape(grid_rows * mode_count, columns)
        sums = jnp.dot(coarse_ref[...], inputs, preferred_element_type=F32)
        sums = sums.reshape(grid_cols, mode_count, columns)
        parting[k][...] = sums.astype(BF16)
        for position, peer in enumerate(col_peers):
            sum_copy(k, peer, peer, col_slots[position]).start()
        partial_ref[...] = sums

        if k + 1 == exchanges:
            for earlier in range(exchanges):
                all_gathers(earlier).wait_send()
                all_sums(earlier).wait_send()
            for direction in range(8):

                @pl.when(inside(direction))
                def _():
                    pltpu.make_async_remote_copy(
                        src_ref=outgoing[0].at[pl.ds(0, exchanges)],
                        dst_ref=incoming[0].at[pl.ds(0, exchanges)],
                        send_sem=halo_send_sem.at[direction],
                        recv_sem=halo_recv_sem.at[0, direction],
                        device_id=neighbour(direction),
                        device_id_type=MESH,
                    ).wait_send()

        for direction in range(8):

            @pl.when(inside(direction))
            def _():
                halo_arrival(k, direction).wait_recv()

        chosen = []
        for s in range(slot_count):
            index = slot_dir[0, 0, s]
            block = incoming[k][jnp.maximum(index, 0)]
            chosen.append(jnp.where(index >= 0, block, jnp.zeros_like(block)))
        coupled = jnp.dot(
            jnp.concatenate(chosen, 1), placed_ref[...], preferred_element_type=F32
        )
        rounded = (rhs_ref[...].astype(F32) - (product + coupled)).astype(BF16)
        if k + 1 < exchanges:
            restrict(k + 1, rounded)
            send_restricted(k + 1)
        local = jnp.dot(rounded, solver_ref[...], preferred_element_type=F32)
        all_sums(k).wait_recv()
        coarse = partial_ref[col]
        for j in range(grid_cols - 1):
            coarse = coarse + arrived[k][j].astype(F32)
        correction = lax.dot_general(
            coarse.astype(BF16),
            modes_ref[...],
            (((0,), (0,)), ((), ())),
            preferred_element_type=F32,
        )
        solution = solution + (local + correction)

    out_ref[0, 0] = solution


def on_device(
    grid_rows,
    grid_cols,
    rhs,
    operator_blocks,
    local_solver,
    modes,
    coupling,
    coarse_inverse,
    send_block,
    slot_dir,
    slot_block,
):
    columns, unknowns = rhs.shape[2:]
    mode_count = modes.shape[2]
    slot_count, block_size = coupling.shape[2:4]
    block_count = unknowns // block_size
    coarse_tile = coarse_inverse[0, :, 0, :].T
    exchanges = ITERS - 1
    blocks = pltpu.VMEM((8, columns, block_size), BF16)
    anywhere = pl.BlockSpec(memory_space=pl.ANY)
    scalars = pl.BlockSpec(memory_space=pltpu.SMEM)
    return pl.pallas_call(
        functools.partial(kernel, grid_rows, grid_cols),
        out_shape=jax.ShapeDtypeStruct((1, 1, columns, unknowns), F32),
        in_specs=[anywhere] * 6 + [scalars] * 3,
        out_specs=pl.BlockSpec(memory_space=pltpu.VMEM),
        scratch_shapes=[
            pltpu.VMEM((columns, unknowns), BF16),
            pltpu.VMEM((unknowns, unknowns), BF16),
            pltpu.VMEM((unknowns, unknowns), BF16),
            pltpu.VMEM((mode_count, unknowns), BF16),
            pltpu.VMEM((slot_count, block_size, block_size), BF16),
            pltpu.VMEM(coarse_tile.shape, BF16),
            pltpu.VMEM((slot_count * block_size, unknowns), BF16),
            pltpu.VMEM((block_count, columns, block_size), BF16),
            pltpu.VMEM((grid_cols, mode_count, columns), F32),
            pltpu.SemaphoreType.DMA((6,)),
            pltpu.SemaphoreType.DMA((8,)),
            pltpu.SemaphoreType.DMA((exchanges, 8)),
            pltpu.SemaphoreType.DMA((exchanges,)),
            pltpu.SemaphoreType.DMA((exchanges,)),
            pltpu.SemaphoreType.DMA((exchanges,)),
            pltpu.SemaphoreType.DMA((exchanges,)),
        ]
        + [blocks] * (2 * exchanges)
        + [pltpu.VMEM((grid_rows, mode_count, columns), BF16)] * exchanges
        + [pltpu.VMEM((grid_cols, mode_count, columns), BF16)] * exchanges
        + [pltpu.VMEM((grid_cols - 1, mode_count, columns), BF16)] * exchanges,
        compiler_params=pltpu.CompilerParams(
            collective_id=0, has_side_effects=True, vmem_limit_bytes=60 * 1024 * 1024
        ),
    )(
        rhs,
        operator_blocks,
        local_solver,
        modes,
        coupling,
        coarse_tile,
        send_block,
        slot_dir,
        slot_block,
    )


def solution(mesh):
    in_specs = (
        P("row", "col", None, None),
        P("row", "col", None, None),
        P("row", "col", None, None),
        P("row", "col", None, None),
        P("row", "col", None, None, None),
        P("col", None, "row", None),
        P("row", "col", None),
        P("row", "col", None),
        P("row", "col", None),
    )
    return jax.shard_map(
        functools.partial(on_device, mesh.shape["row"], mesh.shape["col"]),
        mesh=mesh,
        in_specs=in_specs,
        out_specs=P("row", "col", None, None),
        check_vma=False,
    )
```

```python
import functools

import jax
import jax.numpy as jnp
from jax import lax
from jax.experimental import pallas as pl
from jax.experimental.pallas import tpu as pltpu
from jax.sharding import PartitionSpec as P

ITERS = 6
OFFSETS = ((-1, -1), (-1, 0), (-1, 1), (0, -1), (0, 1), (1, -1), (1, 0), (1, 1))
MESH = pl.DeviceIdType.MESH
F32 = jnp.float32
BF16 = jnp.bfloat16


def kernel(
    grid_rows,
    grid_cols,
    rhs_hbm,
    operator_hbm,
    solver_hbm,
    modes_hbm,
    coupling_hbm,
    coarse_hbm,
    send_block,
    slot_dir,
    slot_block,
    out_ref,
    rhs_ref,
    operator_ref,
    solver_ref,
    modes_ref,
    coupling_ref,
    coarse_ref,
    placed_ref,
    field_ref,
    partial_ref,
    load_sem,
    halo_send_sem,
    halo_recv_sem,
    gather_send_sem,
    gather_recv_sem,
    sum_send_sem,
    sum_recv_sem,
    *slots,
):
    exchanges = ITERS - 1
    outgoing = slots[0:exchanges]
    incoming = slots[exchanges : 2 * exchanges]
    gathered = slots[2 * exchanges : 3 * exchanges]
    parting = slots[3 * exchanges : 4 * exchanges]
    arrived = slots[4 * exchanges : 5 * exchanges]
    row = lax.axis_index("row")
    col = lax.axis_index("col")
    columns, unknowns = rhs_ref.shape
    slot_count, block_size = coupling_ref.shape[0], coupling_ref.shape[1]
    block_count = unknowns // block_size
    mode_count = modes_ref.shape[0]
    packed_rows = gathered[0].shape[1]

    def inside(direction):
        shift_a, shift_b = OFFSETS[direction]
        a, b = row + shift_a, col + shift_b
        return (a >= 0) & (a < grid_rows) & (b >= 0) & (b < grid_cols)

    def neighbour(direction):
        shift_a, shift_b = OFFSETS[direction]
        return (row + shift_a, col + shift_b)

    loads = []
    for i, (source, target) in enumerate(
        (
            (rhs_hbm.at[0, 0], rhs_ref),
            (modes_hbm.at[0, 0], modes_ref),
            (solver_hbm.at[0, 0], solver_ref),
            (operator_hbm.at[0, 0], operator_ref),
            (coarse_hbm, coarse_ref),
            (coupling_hbm.at[0, 0], coupling_ref),
        )
    ):
        load = pltpu.make_async_copy(source, target, load_sem.at[i])
        load.start()
        loads.append(load)

    barrier = pltpu.get_barrier_semaphore()

    def around(index, size):
        steps = sorted(range(1, size), key=lambda step: -min(step, size - step))
        peers = [index + step for step in steps]
        return [jnp.where(peer >= size, peer - size, peer) for peer in peers]

    row_peers = around(row, grid_rows)
    col_peers = around(col, grid_cols)
    col_slots = sorted(range(grid_cols - 1), key=lambda at: -min(at + 1, grid_cols - 1 - at))
    for peer in row_peers:
        pl.semaphore_signal(barrier, inc=1, device_id=(peer, col), device_id_type=MESH)
    for peer in col_peers:
        pl.semaphore_signal(barrier, inc=1, device_id=(row, peer), device_id_type=MESH)
    expected = grid_rows + grid_cols - 2
    for direction in (0, 2, 5, 7):
        there = inside(direction)

        @pl.when(there)
        def _():
            pl.semaphore_signal(
                barrier, inc=1, device_id=neighbour(direction), device_id_type=MESH
            )

        expected = expected + there.astype(jnp.int32)

    def halo_copy(k, direction):
        return pltpu.make_async_remote_copy(
            src_ref=outgoing[k].at[direction],
            dst_ref=incoming[k].at[7 - direction],
            send_sem=halo_send_sem.at[direction],
            recv_sem=halo_recv_sem.at[k, 7 - direction],
            device_id=neighbour(direction),
            device_id_type=MESH,
        )

    def halo_arrival(k, direction):
        return pltpu.make_async_remote_copy(
            src_ref=outgoing[k].at[7 - direction],
            dst_ref=incoming[k].at[direction],
            send_sem=halo_send_sem.at[7 - direction],
            recv_sem=halo_recv_sem.at[k, direction],
            device_id=neighbour(direction),
            device_id_type=MESH,
        )

    def gather_copy(k, peer, slot):
        return pltpu.make_async_remote_copy(
            src_ref=gathered[k].at[slot],
            dst_ref=gathered[k].at[slot],
            send_sem=gather_send_sem.at[k],
            recv_sem=gather_recv_sem.at[k],
            device_id=(peer, col),
            device_id_type=MESH,
        )

    def sum_copy(k, peer, source, slot):
        return pltpu.make_async_remote_copy(
            src_ref=parting[k].at[source],
            dst_ref=arrived[k].at[slot],
            send_sem=sum_send_sem.at[k],
            recv_sem=sum_recv_sem.at[k],
            device_id=(row, peer),
            device_id_type=MESH,
        )

    def all_gathers(k):
        return gather_copy(k, row_peers[0], pl.ds(0, grid_rows - 1))

    def all_sums(k):
        both = pl.ds(0, grid_cols - 1)
        return sum_copy(k, col_peers[0], both, both)

    def restrict(k, rounded):
        restricted = lax.dot_general(
            modes_ref[...], rounded, (((1,), (1,)), ((), ())), preferred_element_type=F32
        )
        restricted = restricted.astype(BF16)
        rest = mode_count - packed_rows
        beside = restricted[packed_rows:]
        if rest < packed_rows:
            beside = jnp.concatenate(
                [beside, jnp.zeros((packed_rows - rest, columns), BF16)], 0
            )
        gathered[k][row] = jnp.concatenate([restricted[:packed_rows], beside], 1)

    def send_restricted(k):
        for peer in row_peers:
            gather_copy(k, peer, row).start()

    loads[0].wait()
    loads[1].wait()
    rhs = rhs_ref[...]
    restrict(0, rhs)
    for direction in range(8):

        @pl.when(jnp.logical_not(inside(direction)))
        def _():
            for k in range(exchanges):
                incoming[k][direction] = jnp.zeros((columns, block_size), BF16)

    pl.semaphore_wait(barrier, expected)
    send_restricted(0)
    loads[5].wait()
    for s in range(slot_count):
        used = slot_dir[0, 0, s] >= 0
        for block in range(block_count):
            here = used & (slot_block[0, 0, s] == block)
            placed_ref[
                s * block_size : (s + 1) * block_size,
                block * block_size : (block + 1) * block_size,
            ] = jnp.where(here, coupling_ref[s], jnp.zeros_like(coupling_ref[s]))
    loads[2].wait()
    solution = jnp.dot(rhs, solver_ref[...], preferred_element_type=F32)

    for k in range(exchanges):
        field = solution.astype(BF16)
        for block in range(block_count):
            field_ref[block] = field[:, block * block_size : (block + 1) * block_size]
        for direction in range(8):
            outgoing[k][direction] = field_ref[send_block[0, 0, direction]]
        for direction in (1, 6, 0, 2, 5, 7, 3, 4):

            @pl.when(inside(direction))
            def _():
                halo_copy(k, direction).start()

        if k == 0:
            loads[3].wait()
            loads[4].wait()
        product = jnp.dot(field, operator_ref[...], preferred_element_type=F32)

        all_gathers(k).wait_recv()
        packed = gathered[k][...]
        first = packed[:, :, :columns]
        second = packed[:, : mode_count - packed_rows, columns:]
        inputs = jnp.concatenate([first, second], 1).reshape(grid_rows * mode_count, columns)
        sums = jnp.dot(coarse_ref[...], inputs, preferred_element_type=F32)
        sums = sums.reshape(grid_cols, mode_count, columns)
        parting[k][...] = sums.astype(BF16)
        for position, peer in enumerate(col_peers):
            sum_copy(k, peer, peer, col_slots[position]).start()
        partial_ref[...] = sums

        if k + 1 == exchanges:
            for earlier in range(exchanges):
                all_gathers(earlier).wait_send()
                all_sums(earlier).wait_send()
            for direction in range(8):

                @pl.when(inside(direction))
                def _():
                    pltpu.make_async_remote_copy(
                        src_ref=outgoing[0].at[pl.ds(0, exchanges)],
                        dst_ref=incoming[0].at[pl.ds(0, exchanges)],
                        send_sem=halo_send_sem.at[direction],
                        recv_sem=halo_recv_sem.at[0, direction],
                        device_id=neighbour(direction),
                        device_id_type=MESH,
                    ).wait_send()

        for direction in range(8):

            @pl.when(inside(direction))
            def _():
                halo_arrival(k, direction).wait_recv()

        chosen = []
        for s in range(slot_count):
            index = slot_dir[0, 0, s]
            block = incoming[k][jnp.maximum(index, 0)]
            chosen.append(jnp.where(index >= 0, block, jnp.zeros_like(block)))
        coupled = jnp.dot(
            jnp.concatenate(chosen, 1), placed_ref[...], preferred_element_type=F32
        )
        rounded = (rhs_ref[...].astype(F32) - (product + coupled)).astype(BF16)
        if k + 1 < exchanges:
            restrict(k + 1, rounded)
            send_restricted(k + 1)
        local = jnp.dot(rounded, solver_ref[...], preferred_element_type=F32)
        all_sums(k).wait_recv()
        coarse = partial_ref[col]
        for j in range(grid_cols - 1):
            coarse = coarse + arrived[k][j].astype(F32)
        correction = lax.dot_general(
            coarse.astype(BF16),
            modes_ref[...],
            (((0,), (0,)), ((), ())),
            preferred_element_type=F32,
        )
        solution = solution + (local + correction)

    out_ref[0, 0] = solution


def on_device(
    grid_rows,
    grid_cols,
    rhs,
    operator_blocks,
    local_solver,
    modes,
    coupling,
    coarse_inverse,
    send_block,
    slot_dir,
    slot_block,
):
    columns, unknowns = rhs.shape[2:]
    mode_count = modes.shape[2]
    slot_count, block_size = coupling.shape[2:4]
    block_count = unknowns // block_size
    coarse_tile = coarse_inverse[0, :, 0, :].T
    packed_rows = pl.cdiv(mode_count, 32) * 16
    exchanges = ITERS - 1
    blocks = pltpu.VMEM((8, columns, block_size), BF16)
    anywhere = pl.BlockSpec(memory_space=pl.ANY)
    scalars = pl.BlockSpec(memory_space=pltpu.SMEM)
    return pl.pallas_call(
        functools.partial(kernel, grid_rows, grid_cols),
        out_shape=jax.ShapeDtypeStruct((1, 1, columns, unknowns), F32),
        in_specs=[anywhere] * 6 + [scalars] * 3,
        out_specs=pl.BlockSpec(memory_space=pltpu.VMEM),
        scratch_shapes=[
            pltpu.VMEM((columns, unknowns), BF16),
            pltpu.VMEM((unknowns, unknowns), BF16),
            pltpu.VMEM((unknowns, unknowns), BF16),
            pltpu.VMEM((mode_count, unknowns), BF16),
            pltpu.VMEM((slot_count, block_size, block_size), BF16),
            pltpu.VMEM(coarse_tile.shape, BF16),
            pltpu.VMEM((slot_count * block_size, unknowns), BF16),
            pltpu.VMEM((block_count, columns, block_size), BF16),
            pltpu.VMEM((grid_cols, mode_count, columns), F32),
            pltpu.SemaphoreType.DMA((6,)),
            pltpu.SemaphoreType.DMA((8,)),
            pltpu.SemaphoreType.DMA((exchanges, 8)),
            pltpu.SemaphoreType.DMA((exchanges,)),
            pltpu.SemaphoreType.DMA((exchanges,)),
            pltpu.SemaphoreType.DMA((exchanges,)),
            pltpu.SemaphoreType.DMA((exchanges,)),
        ]
        + [blocks] * (2 * exchanges)
        + [pltpu.VMEM((grid_rows, packed_rows, 2 * columns), BF16)] * exchanges
        + [pltpu.VMEM((grid_cols, mode_count, columns), BF16)] * exchanges
        + [pltpu.VMEM((grid_cols - 1, mode_count, columns), BF16)] * exchanges,
        compiler_params=pltpu.CompilerParams(
            collective_id=0, has_side_effects=True, vmem_limit_bytes=60 * 1024 * 1024
        ),
    )(
        rhs,
        operator_blocks,
        local_solver,
        modes,
        coupling,
        coarse_tile,
        send_block,
        slot_dir,
        slot_block,
    )


def solution(mesh):
    in_specs = (
        P("row", "col", None, None),
        P("row", "col", None, None),
        P("row", "col", None, None),
        P("row", "col", None, None),
        P("row", "col", None, None, None),
        P("col", None, "row", None),
        P("row", "col", None),
        P("row", "col", None),
        P("row", "col", None),
    )
    return jax.shard_map(
        functools.partial(on_device, mesh.shape["row"], mesh.shape["col"]),
        mesh=mesh,
        in_specs=in_specs,
        out_specs=P("row", "col", None, None),
        check_vma=False,
    )
```
